32 devices in a mesh: batch: 2 (over y), row: 16 (over z, x, core).
Axes of the slice: x: 2, y: 2, z: 4, core: 2. Of those that a mesh axis runs over, the one named last changes fastest.
Arguments:
- tensor: float32 [128, 3, 4, 128, 128], P(('batch', 'row')), parts along dimension 0, may hold values from -0.5 to 0.5
- density: float32 [128, 5, 128, 128], P(('batch', 'row')), parts along dimension 0, as said below
- metric: float32 [8, 4], P('batch'), parts along dimension 0, as said below
- offsets: int32 [128, 3], P('batch'), parts along dimension 0, may hold values from -2 to 2, as said below
- counts: int32 [128], P('batch'), parts along dimension 0, may hold values from 1 to 3, as said below
Outputs:
- exchange: float32 [128, 5, 128, 128], P(('batch', 'row')), parts along dimension 0
The draws below stay inside these ranges and needn't reach their ends.
There are 2 independent parts, one for each index of `batch`. The reference program is written for one: setup_inputs(seed, part) draws one part's arguments, and reference() takes and returns one part's arrays. A program takes and returns all parts, laid end to end along the dimension named above; each array names one. Nothing has to cross between parts.
Inputs may be any that keep to these rules, and one draw needn't show every extreme that they name: Each row holds 3 different offsets. Slots from counts[m] on are padding. density is symmetric: density[l, k] is the transpose of density[l + k - 2, 4 - k], block indices modulo 64. metric is symmetric.
All inputs are finite; a program needn't handle non-finite values.
Results may differ from the reference program's by a relative error of at most 0.0003.
Values sent between devices are 32-bit elements; how exact they have to be, the bound alone decides.
A program may use at most 128 MiB of HBM per device.

```python
import math
import jax
import jax.numpy as jnp
from jax import lax

BASIS_PER_BLOCK = 128
BLOCK_RADIUS = 2
PARTNER_SLOTS = 3
AUX_FUNCTIONS = 4
CELL_BLOCKS = 64


def draw_density(key, part):
    key = jax.random.fold_in(key, 11)
    width = 2 * BLOCK_RADIUS + 1
    raw = 1.27 * jax.random.normal(key, (CELL_BLOCKS, width, BASIS_PER_BLOCK, BASIS_PER_BLOCK), jnp.float32) / math.sqrt(BASIS_PER_BLOCK)
    rows = (jnp.arange(CELL_BLOCKS)[:, None] + jnp.arange(width)[None, :] - BLOCK_RADIUS) % CELL_BLOCKS
    cols = jnp.broadcast_to((width - 1 - jnp.arange(width))[None, :], rows.shape)
    partner = jnp.swapaxes(raw[rows, cols], -1, -2)
    return 0.5 * (raw + partner)


def draw_metric(key, part):
    key = jax.random.fold_in(key, 12)
    raw = jax.random.normal(key, (AUX_FUNCTIONS, AUX_FUNCTIONS), jnp.float32)
    return jnp.eye(AUX_FUNCTIONS, dtype=jnp.float32) + 0.25 * (raw + raw.T) / math.sqrt(AUX_FUNCTIONS)


def draw_offsets(key, part):
    key = jax.random.fold_in(key, 13)
    width = 2 * BLOCK_RADIUS + 1
    scores = jax.random.randint(key, (CELL_BLOCKS, width), 0, 4096) * width + jnp.arange(width)[None, :]
    sorted_order = jnp.argsort(scores, axis=1)
    return (sorted_order[:, :PARTNER_SLOTS] - BLOCK_RADIUS).astype(jnp.int32)


def draw_counts(key, part):
    key = jax.random.fold_in(key, 14)
    leading_key, second_key = jax.random.split(key)
    sampled_values = jax.random.randint(leading_key, (CELL_BLOCKS,), 1, PARTNER_SLOTS + 1)
    chosen_partners = jax.random.randint(second_key, (), 0, CELL_BLOCKS)
    return jnp.where(jnp.arange(CELL_BLOCKS) == chosen_partners, PARTNER_SLOTS, sampled_values).astype(jnp.int32)


def shard_levels(own_key, extent, shards, smallest, largest):
    factor_of, own = 1.0, jax.random.fold_in(own_key, 6)
    for position, parts in shards:
        draws = jnp.exp(jax.random.uniform(jax.random.fold_in(own, position), (parts,), jnp.float32, smallest / len(shards), largest / len(shards)))
        factor_of = factor_of * jnp.repeat(draws, extent[position] // parts).reshape([-1 if axis == position else 1 for axis in range(len(extent))])
    return factor_of


def centred(own_key, shape, spread, reach, shards=(), kind=jnp.bfloat16):
    values = jax.random.normal(own_key, shape, jnp.float32) * spread
    if len(shards) > 0:
        values = shard_levels(own_key, shape, shards, -0.22, 0.18) * values
    return jnp.clip(values, min=-reach, max=reach).astype(kind)


def setup_inputs(seed: int = 0, part: int = 0) -> dict:
    arg_keys = jax.random.split(jax.random.key(seed), 6)
    own_keys = jax.random.split(jax.random.fold_in(arg_keys[5], part), 6)
    return {
        "tensor": centred(own_keys[0], (CELL_BLOCKS, PARTNER_SLOTS, AUX_FUNCTIONS, BASIS_PER_BLOCK, BASIS_PER_BLOCK), BASIS_PER_BLOCK ** -0.5, 0.5, ((0, 16),), jnp.float32),
        "density": draw_density(jax.random.fold_in(jax.random.fold_in(arg_keys[5], part), 71), part),
        "metric": draw_metric(jax.random.fold_in(jax.random.fold_in(arg_keys[5], part), 71), part),
        "offsets": draw_offsets(jax.random.fold_in(jax.random.fold_in(arg_keys[5], part), 71), part),
        "counts": draw_counts(jax.random.fold_in(jax.random.fold_in(arg_keys[5], part), 71), part),
    }


def reference(tensor, density, metric, offsets, counts):
    high = lax.Precision.HIGHEST
    width = 2 * BLOCK_RADIUS + 1
    active_mask = (jnp.arange(PARTNER_SLOTS, dtype=jnp.int32)[None, :] < counts[:, None]).astype(jnp.float32)

    def one_block(block):
        inner = jnp.zeros((AUX_FUNCTIONS, 4 * BLOCK_RADIUS + 1, BASIS_PER_BLOCK, BASIS_PER_BLOCK), jnp.float32)
        for slot_position in range(PARTNER_SLOTS):
            offset = offsets[block, slot_position]
            partner = ((block + offset) % CELL_BLOCKS).astype(jnp.int32)
            dens_rows = lax.dynamic_index_in_dim(density, partner, 0, keepdims=False)
            masked = tensor[block, slot_position] * active_mask[block, slot_position]
            terms = jnp.einsum("pab,kbc->pkac", masked, dens_rows, precision=high)
            start = (offset + BLOCK_RADIUS).astype(jnp.int32)
            window = lax.dynamic_slice_in_dim(inner, start, width, 1)
            inner = lax.dynamic_update_slice_in_dim(inner, window + terms, start, 1)
        contracted = jnp.einsum("qp,poac->qoac", metric, inner, precision=high)
        result = []
        for shift_q in range(-BLOCK_RADIUS, BLOCK_RADIUS + 1):
            neighbour = ((block + shift_q) % CELL_BLOCKS).astype(jnp.int32)
            neigh_ten = lax.dynamic_index_in_dim(tensor, neighbour, 0, keepdims=False)
            neigh_off = lax.dynamic_index_in_dim(offsets, neighbour, 0, keepdims=False)
            neigh_live = lax.dynamic_index_in_dim(active_mask, neighbour, 0, keepdims=False)
            summed = jnp.zeros((BASIS_PER_BLOCK, BASIS_PER_BLOCK), jnp.float32)
            for slot_position in range(PARTNER_SLOTS):
                place = (shift_q + neigh_off[slot_position] + 2 * BLOCK_RADIUS).astype(jnp.int32)
                e_block = lax.dynamic_index_in_dim(contracted, place, 1, keepdims=False)
                summed = summed + jnp.einsum("qac,qbc->ab", e_block, neigh_ten[slot_position] * neigh_live[slot_position], precision=high)
            result.append(summed)
        return jnp.stack(result)

    return lax.map(one_block, jnp.arange(CELL_BLOCKS, dtype=jnp.int32))
```

```python
import functools

import jax
import jax.numpy as jnp
from jax import lax
from jax.experimental import pallas as pl
from jax.experimental.pallas import tpu as pltpu
from jax.sharding import PartitionSpec as P

MESH = pl.DeviceIdType.MESH
F32 = jnp.float32
BF16 = jnp.bfloat16
RADIUS = 2
WIDTH = 2 * RADIUS + 1
BLOCKS = 4
SLOTS = 3
AUX = 4
B = 128
ZERO = 8 * WIDTH
COLS = 13


def split(x):
    hi = x.astype(BF16)
    return hi, (x - hi.astype(F32)).astype(BF16)


def dot(a, b):
    return jnp.dot(a, b, preferred_element_type=F32)


def dot_t(a, b):
    return lax.dot_general(a, b, (((1,), (1,)), ((), ())), preferred_element_type=F32)


def kernel(
    ring,
    ten_hbm,
    den_hbm,
    metric,
    offsets,
    counts,
    out,
    ten,
    den,
    den_l3,
    den_l2,
    den_r0,
    den_r1,
    ten_l,
    ten_r,
    d_hi,
    d_lo,
    v_hi,
    v_lo,
    u_hi,
    u_lo,
    e_hi,
    e_lo,
    to_right,
    to_left,
    from_left,
    from_right,
    local_sem,
    send_sem,
    recv_sem,
):
    me = lax.axis_index("row")
    right = lax.rem(me + 1, ring)
    left = lax.rem(me + ring - 1, ring)
    total = ring * BLOCKS
    first = me * BLOCKS

    own_ten = pltpu.make_async_copy(ten_hbm, ten, local_sem.at[0])
    own_den = pltpu.make_async_copy(den_hbm, den, local_sem.at[1])
    own_den.start()
    own_ten.start()

    barrier = pltpu.get_barrier_semaphore()
    for side in (left, right):
        pl.semaphore_signal(barrier, inc=1, device_id={"row": side}, device_id_type=MESH)
    pl.semaphore_wait(barrier, 2)

    def remote(src, dst, number, side):
        return pltpu.make_async_remote_copy(
            src_ref=src,
            dst_ref=dst,
            send_sem=send_sem.at[number],
            recv_sem=recv_sem.at[number],
            device_id={"row": side},
            device_id_type=MESH,
        )

    den_moves = [
        remote(den_hbm.at[3, 0:3], den_l3, 0, right),
        remote(den_hbm.at[0, 2:5], den_r0, 1, left),
        remote(den_hbm.at[2, 2], den_l2, 2, right),
        remote(den_hbm.at[1, 2:4], den_r1, 3, left),
    ]
    ten_moves = [
        remote(ten_hbm.at[0], ten_r, 4, left),
        remote(ten_hbm.at[3], ten_l, 5, right),
    ]
    for move in den_moves + ten_moves:
        move.start()

    def block_offset(n, s):
        return offsets[lax.rem(first + n + total, total), s]

    def block_live(n, s):
        return jnp.where(s < counts[lax.rem(first + n + total, total)], 1.0, 0.0).astype(F32)

    def put(i, k, block):
        hi, lo = split(block)
        d_hi[(i + RADIUS) * WIDTH + k] = hi
        d_lo[(i + RADIUS) * WIDTH + k] = lo

    own_den.wait()
    for number in (0, 1, 7 * WIDTH + 4, ZERO):
        d_hi[number] = jnp.zeros((B, B), BF16)
        d_lo[number] = jnp.zeros((B, B), BF16)

    def own_rows(step, carry):
        hi, lo = split(den[step])
        at = pl.ds((step + RADIUS) * WIDTH, WIDTH)
        d_hi[at] = hi
        d_lo[at] = lo
        return carry

    lax.fori_loop(0, BLOCKS, own_rows, 0)
    for i, j in ((-1, 0), (-1, 1), (-2, 0), (4, 2), (4, 3), (5, 3)):
        put(i, j - i + RADIUS, den[j, i - j + RADIUS].T)

    own_ten.wait()

    def prepare(m, carry):
        for s in range(SLOTS):
            live = block_live(m, s)
            parts = [ten[m, s, p] * live for p in range(AUX)]
            for q in range(AUX):
                hi, lo = split(parts[q])
                u_hi[m, s, :, q * B : (q + 1) * B] = hi
                u_lo[m, s, :, q * B : (q + 1) * B] = lo
                mixed = metric[q, 0] * parts[0]
                for p in range(1, AUX):
                    mixed = mixed + metric[q, p] * parts[p]
                hi, lo = split(mixed)
                v_hi[m, q * B : (q + 1) * B, s * B : (s + 1) * B] = hi
                v_lo[m, q * B : (q + 1) * B, s * B : (s + 1) * B] = lo
        return carry

    lax.fori_loop(0, BLOCKS, prepare, 0)

    for move in den_moves:
        move.wait_recv()
    for k in range(3):
        put(-1, k, den_l3[k])
        put(4, k + 2, den_r0[k])
    put(-2, 2, den_l2[...])
    put(-2, 3, den_l3[1].T)
    put(5, 1, den_r0[1].T)
    put(5, 2, den_r1[0])
    put(5, 3, den_r1[1])

    def half(m, o):
        rows_hi, rows_lo = [], []
        for s in range(SLOTS):
            shift = block_offset(m, s)
            pair_hi, pair_lo = [], []
            for step in (0, 1):
                k = o + step - shift + RADIUS
                at = jnp.where(
                    jnp.logical_and(k >= 0, k < WIDTH),
                    (m + shift + RADIUS) * WIDTH + k,
                    ZERO,
                )
                pair_hi.append(d_hi[at])
                pair_lo.append(d_lo[at])
            rows_hi.append(jnp.concatenate(pair_hi, axis=1))
            rows_lo.append(jnp.concatenate(pair_lo, axis=1))
        right_hi = jnp.concatenate(rows_hi, axis=0)
        right_lo = jnp.concatenate(rows_lo, axis=0)
        left_hi = v_hi[m]
        result = dot(left_hi, right_hi) + (dot(left_hi, right_lo) + dot(v_lo[m], right_hi))
        rows = pl.ds(pl.multiple_of(m * B, B), B)
        for step in (0, 1):
            for q in range(AUX):
                hi, lo = split(result[q * B : (q + 1) * B, step * B : (step + 1) * B])
                e_hi[m + o + step + 4, rows, q * B : (q + 1) * B] = hi
                e_lo[m + o + step + 4, rows, q * B : (q + 1) * B] = lo

    def all_halves(number, carry):
        half(number // 4, (number % 4) * 2 - 2)
        return carry

    lax.fori_loop(0, 4 * BLOCKS, all_halves, 0)
    half(1, -4)

    def close(n, start, stop, part_hi, part_lo):
        result = jnp.zeros(((stop - start) * B, B), F32)
        for s in range(SLOTS):
            at = n + block_offset(n, s) + 4
            left_hi = e_hi[at, start * B : stop * B, :]
            left_lo = e_lo[at, start * B : stop * B, :]
            right_hi, right_lo = part_hi(s), part_lo(s)
            result = result + (
                dot_t(left_hi, right_hi) + (dot_t(left_hi, right_lo) + dot_t(left_lo, right_hi))
            )
        return [result[i * B : (i + 1) * B] for i in range(stop - start)]

    for n in range(BLOCKS):
        start = max(0, n - RADIUS)
        found = close(n, start, n + 1, lambda s: u_hi[n, s], lambda s: u_lo[n, s])
        for m in range(start, n + 1):
            block = found[m - start]
            out[m, n - m + RADIUS] = block
            if m < n:
                out[n, m - n + RADIUS] = block.T

    def arrived(buffer, n):
        def one(s):
            live = block_live(n, s)
            pieces = [split(buffer[s, q] * live) for q in range(AUX)]
            return [jnp.concatenate([piece[i] for piece in pieces], axis=1) for i in (0, 1)]

        both = [one(s) for s in range(SLOTS)]
        return (lambda s: both[s][0]), (lambda s: both[s][1])

    answer_right = remote(to_right, from_left, 6, right)
    answer_left = remote(to_left, from_right, 7, left)

    ten_moves[0].wait_recv()
    found = close(4, 2, 4, *arrived(ten_r, 4))
    for i in (0, 1):
        to_right[i] = found[i].T
    answer_right.start()
    for i in (0, 1):
        out[2 + i, 4 - i] = found[i]

    ten_moves[1].wait_recv()
    found = close(-1, 1, 2, *arrived(ten_l, -1))
    to_left[...] = found[0].T
    answer_left.start()
    out[1, 0] = found[0]

    answer_right.wait_recv()
    out[0, 0] = from_left[0]
    out[0, 1] = from_left[1]
    answer_left.wait_recv()
    out[3, 4] = from_right[...]
    for move in den_moves + ten_moves + [answer_right, answer_left]:
        move.wait_send()


def body(tensor, density, metric, offsets, counts):
    ring = lax.axis_size("row")
    any_space = pl.BlockSpec(memory_space=pl.ANY)
    smem = pl.BlockSpec(memory_space=pltpu.SMEM)
    return pl.pallas_call(
        functools.partial(kernel, ring),
        out_shape=jax.ShapeDtypeStruct(density.shape, F32),
        in_specs=[any_space, any_space, smem, smem, smem],
        out_specs=pl.BlockSpec(memory_space=pltpu.VMEM),
        scratch_shapes=[
            pltpu.VMEM((BLOCKS, SLOTS, AUX, B, B), F32),
            pltpu.VMEM((BLOCKS, WIDTH, B, B), F32),
            pltpu.VMEM((3, B, B), F32),
            pltpu.VMEM((B, B), F32),
            pltpu.VMEM((3, B, B), F32),
            pltpu.VMEM((2, B, B), F32),
            pltpu.VMEM((SLOTS, AUX, B, B), F32),
            pltpu.VMEM((SLOTS, AUX, B, B), F32),
            pltpu.VMEM((ZERO + 1, B, B), BF16),
            pltpu.VMEM((ZERO + 1, B, B), BF16),
            pltpu.VMEM((BLOCKS, AUX * B, SLOTS * B), BF16),
            pltpu.VMEM((BLOCKS, AUX * B, SLOTS * B), BF16),
            pltpu.VMEM((BLOCKS, SLOTS, B, AUX * B), BF16),
            pltpu.VMEM((BLOCKS, SLOTS, B, AUX * B), BF16),
            pltpu.VMEM((COLS, BLOCKS * B, AUX * B), BF16),
            pltpu.VMEM((COLS, BLOCKS * B, AUX * B), BF16),
            pltpu.VMEM((2, B, B), F32),
            pltpu.VMEM((B, B), F32),
            pltpu.VMEM((2, B, B), F32),
            pltpu.VMEM((B, B), F32),
            pltpu.SemaphoreType.DMA((2,)),
            pltpu.SemaphoreType.DMA((8,)),
            pltpu.SemaphoreType.DMA((8,)),
        ],
        compiler_params=pltpu.CompilerParams(
            collective_id=0, has_side_effects=True, vmem_limit_bytes=48 * 1024 * 1024
        ),
        cost_estimate=pl.CostEstimate(flops=6 * 10**9, bytes_accessed=6 * 10**6, transcendentals=0),
    )(tensor, density, metric, offsets, counts)


def solution(mesh):
    return jax.shard_map(
        body,
        mesh=mesh,
        in_specs=(
            P(("batch", "row"), None, None, None, None),
            P(("batch", "row"), None, None, None),
            P("batch", None),
            P("batch", None),
            P("batch"),
        ),
        out_specs=P(("batch", "row"), None, None, None),
        check_vma=False,
    )
```

```python
import functools

import jax
import jax.numpy as jnp
from jax import lax
from jax.experimental import pallas as pl
from jax.experimental.pallas import tpu as pltpu
from jax.sharding import PartitionSpec as P

MESH = pl.DeviceIdType.MESH
F32 = jnp.float32
BF16 = jnp.bfloat16
RADIUS = 2
WIDTH = 2 * RADIUS + 1
BLOCKS = 4
SLOTS = 3
AUX = 4
B = 128
ZERO = 8 * WIDTH
CHUNKS = 2
ROWS = B // CHUNKS
COLS = 13


def split(x):
    hi = x.astype(BF16)
    return hi, (x - hi.astype(F32)).astype(BF16)


def dot(a, b):
    return jnp.dot(a, b, preferred_element_type=F32)


def dot_t(a, b):
    return lax.dot_general(a, b, (((1,), (1,)), ((), ())), preferred_element_type=F32)


def kernel(
    ring,
    ten_hbm,
    den_hbm,
    metric_hbm,
    offsets_hbm,
    counts_hbm,
    out,
    metric,
    offsets,
    counts,
    ten,
    den,
    den_l3,
    den_l2,
    den_r0,
    den_r1,
    ten_l,
    ten_r,
    d_hi,
    d_lo,
    v,
    u_hi,
    u_lo,
    e_hi,
    e_lo,
    to_right,
    to_left,
    from_left,
    from_right,
    local_sem,
    send_sem,
    recv_sem,
):
    me = lax.axis_index("row")
    right = lax.rem(me + 1, ring)
    left = lax.rem(me + ring - 1, ring)
    total = ring * BLOCKS
    first = me * BLOCKS

    own_ten = pltpu.make_async_copy(ten_hbm, ten, local_sem.at[0])
    own_den = pltpu.make_async_copy(den_hbm, den, local_sem.at[1])
    small = [
        pltpu.make_async_copy(src, dst, local_sem.at[2 + i])
        for i, (src, dst) in enumerate(
            ((metric_hbm, metric), (offsets_hbm, offsets), (counts_hbm, counts))
        )
    ]
    for move in small:
        move.start()
    own_den.start()
    own_ten.start()

    barrier = pltpu.get_barrier_semaphore()
    for side in (left, right):
        pl.semaphore_signal(barrier, inc=1, device_id={"row": side}, device_id_type=MESH)
    pl.semaphore_wait(barrier, 2)

    def remote(src, dst, number, side):
        return pltpu.make_async_remote_copy(
            src_ref=src,
            dst_ref=dst,
            send_sem=send_sem.at[number],
            recv_sem=recv_sem.at[number],
            device_id={"row": side},
            device_id_type=MESH,
        )

    den_moves = [
        remote(den_hbm.at[3, 0:3], den_l3, 0, right),
        remote(den_hbm.at[0, 2:5], den_r0, 1, left),
        remote(den_hbm.at[2, 2], den_l2, 2, right),
        remote(den_hbm.at[1, 2:4], den_r1, 3, left),
    ]
    rows_of = [pl.ds(c * ROWS, ROWS) for c in range(CHUNKS)]
    ten_moves = [
        [
            remote(ten_hbm.at[0, :, :, rows_of[c]], ten_r.at[:, :, rows_of[c]], 4 + 4 * c, left),
            remote(ten_hbm.at[3, :, :, rows_of[c]], ten_l.at[:, :, rows_of[c]], 5 + 4 * c, right),
        ]
        for c in range(CHUNKS)
    ]
    for move in den_moves:
        move.start()
    for pair in ten_moves:
        for move in pair:
            move.start()
    answers = [
        [
            remote(to_right.at[:, rows_of[c]], from_left.at[:, rows_of[c]], 6 + 4 * c, right),
            remote(to_left.at[rows_of[c]], from_right.at[rows_of[c]], 7 + 4 * c, left),
        ]
        for c in range(CHUNKS)
    ]

    def block_offset(n, s):
        return offsets[s, lax.rem(first + n + total, total)]

    def block_live(n, s):
        return jnp.where(s < counts[lax.rem(first + n + total, total)], 1.0, 0.0).astype(F32)

    def put(i, k, block):
        hi, lo = split(block)
        d_hi[(i + RADIUS) * WIDTH + k] = hi
        d_lo[(i + RADIUS) * WIDTH + k] = lo

    own_den.wait()
    for number in (0, 1, 2, 3, 5, 6, 7, 32, 33, 34, 36, 37, 38, 39, ZERO):
        d_hi[number] = jnp.zeros((B, B), BF16)
        d_lo[number] = jnp.zeros((B, B), BF16)

    def own_rows(step, carry):
        hi, lo = split(den[step])
        at = pl.ds((step + RADIUS) * WIDTH, WIDTH)
        d_hi[at] = hi
        d_lo[at] = lo
        return carry

    lax.fori_loop(0, BLOCKS, own_rows, 0)
    for i, j in ((-1, 0), (-1, 1), (-2, 0), (4, 2), (4, 3), (5, 3)):
        put(i, j - i + RADIUS, den[j, i - j + RADIUS].T)

    own_ten.wait()
    for move in small:
        move.wait()

    def prepare(m, carry):
        for s in range(SLOTS):
            live = block_live(m, s)
            parts = [ten[m, s, p] * live for p in range(AUX)]
            for q in range(AUX):
                hi, lo = split(parts[q])
                u_hi[m, s, :, q * B : (q + 1) * B] = hi
                u_lo[m, s, :, q * B : (q + 1) * B] = lo
                mixed = metric[q, 0] * parts[0]
                for p in range(1, AUX):
                    mixed = mixed + metric[q, p] * parts[p]
                hi, lo = split(mixed)
                v[m, s, 0, q * B : (q + 1) * B] = hi
                v[m, s, 1, q * B : (q + 1) * B] = lo
        v[m, SLOTS] = jnp.zeros((2, AUX * B, B), BF16)
        return carry

    lax.fori_loop(0, BLOCKS, prepare, 0)

    def half(m, o):
        rows_hi, rows_lo = [], []
        for s in range(SLOTS):
            shift = block_offset(m, s)
            pair_hi, pair_lo = [], []
            for step in (0, 1):
                k = o + step - shift + RADIUS
                at = jnp.where(
                    jnp.logical_and(k >= 0, k < WIDTH),
                    (m + shift + RADIUS) * WIDTH + k,
                    ZERO,
                )
                pair_hi.append(d_hi[at])
                pair_lo.append(d_lo[at])
            rows_hi.append(jnp.concatenate(pair_hi, axis=1))
            rows_lo.append(jnp.concatenate(pair_lo, axis=1))
        left_hi = [v[m, s, 0] for s in range(SLOTS)]
        left_lo = [v[m, s, 1] for s in range(SLOTS)]
        result = dot(
            jnp.concatenate(left_hi + left_hi + left_lo, axis=1),
            jnp.concatenate(rows_hi + rows_lo + rows_hi, axis=0),
        )
        rows = pl.ds(pl.multiple_of(m * B, B), B)
        for step in (0, 1):
            for q in range(AUX):
                hi, lo = split(result[q * B : (q + 1) * B, step * B : (step + 1) * B])
                e_hi[m + o + step + 4, rows, q * B : (q + 1) * B] = hi
                e_lo[m + o + step + 4, rows, q * B : (q + 1) * B] = lo

    def all_halves(number, carry):
        half(number // 4, (number % 4) * 2 - 2)
        return carry

    lax.fori_loop(0, 4 * BLOCKS, all_halves, 0)
    half(1, -4)

    def slot_at(m, shift):
        at = SLOTS
        for s in range(SLOTS):
            at = jnp.where(block_offset(m, s) == shift, s, at)
        return at

    def add_half(m, shifts, columns, blocks):
        ats = [slot_at(m, shift) for shift in shifts]
        left_hi = [v[m, at, 0] for at in ats]
        left_lo = [v[m, at, 1] for at in ats]
        rows_hi = [jnp.concatenate([b[0] for b in row], axis=1) for row in blocks]
        rows_lo = [jnp.concatenate([b[1] for b in row], axis=1) for row in blocks]
        result = dot(
            jnp.concatenate(left_hi + left_hi + left_lo, axis=1),
            jnp.concatenate(rows_hi + rows_lo + rows_hi, axis=0),
        )
        rows = slice(m * B, (m + 1) * B)
        for step, j in enumerate(columns):
            for q in range(AUX):
                lanes = slice(q * B, (q + 1) * B)
                old = e_hi[j + 4, rows, lanes].astype(F32) + e_lo[j + 4, rows, lanes].astype(F32)
                hi, lo = split(old + result[lanes, step * B : (step + 1) * B])
                e_hi[j + 4, rows, lanes] = hi
                e_lo[j + 4, rows, lanes] = lo

    for move in den_moves:
        move.wait_recv()
    row_l1 = [split(den_l3[k]) for k in range(3)]
    row_l2 = [split(den_l2[...]), split(den_l3[1].T)]
    add_half(0, (-1, -2), (-2, -1), [row_l1[1:], row_l2])
    add_half(1, (-2,), (-3, -2, -1), [row_l1])
    row_r0 = [split(den_r0[k]) for k in range(3)]
    row_r1 = [split(den_r0[1].T), split(den_r1[0]), split(den_r1[1])]
    add_half(2, (2,), (4, 5, 6), [row_r0])
    add_half(3, (1, 2), (4, 5, 6), [row_r0, row_r1])

    def close(n, start, stop, part_hi, part_lo):
        result = jnp.zeros(((stop - start) * B, B), F32)
        for s in range(SLOTS):
            at = n + block_offset(n, s) + 4
            left_hi = e_hi[at, start * B : stop * B, :]
            left_lo = e_lo[at, start * B : stop * B, :]
            right_hi, right_lo = part_hi(s), part_lo(s)
            result = result + (
                dot_t(left_hi, right_hi) + (dot_t(left_hi, right_lo) + dot_t(left_lo, right_hi))
            )
        return [result[i * B : (i + 1) * B] for i in range(stop - start)]

    for n in range(BLOCKS):
        start = max(0, n - RADIUS)
        found = close(n, start, n + 1, lambda s: u_hi[n, s], lambda s: u_lo[n, s])
        for m in range(start, n + 1):
            block = found[m - start]
            out[m, n - m + RADIUS] = block
            if m < n:
                out[n, m - n + RADIUS] = block.T

    def close_arrived(buffer, n, start, stop, rows):
        result = jnp.zeros((ROWS, (stop - start) * B), F32)
        for s in range(SLOTS):
            live = block_live(n, s)
            pieces = [split(buffer[s, q, rows] * live) for q in range(AUX)]
            left_hi, left_lo = [
                jnp.concatenate([piece[i] for piece in pieces], axis=1) for i in (0, 1)
            ]
            at = n + block_offset(n, s) + 4
            right_hi = e_hi[at, start * B : stop * B, :]
            right_lo = e_lo[at, start * B : stop * B, :]
            result = result + (
                dot_t(left_hi, right_hi) + (dot_t(left_hi, right_lo) + dot_t(left_lo, right_hi))
            )
        return [result[:, i * B : (i + 1) * B] for i in range(stop - start)]

    for c in range(CHUNKS):
        rows = slice(c * ROWS, (c + 1) * ROWS)
        ten_moves[c][0].wait_recv()
        found = close_arrived(ten_r, 4, 2, 4, rows)
        for i in (0, 1):
            to_right[i, rows] = found[i]
        answers[c][0].start()
        ten_moves[c][1].wait_recv()
        (found,) = close_arrived(ten_l, -1, 1, 2, rows)
        to_left[rows] = found
        answers[c][1].start()

    for i in (0, 1):
        out[2 + i, 4 - i] = to_right[i].T
    out[1, 0] = to_left[...].T

    for pair in answers:
        for move in pair:
            move.wait_recv()
    out[0, 0] = from_left[0]
    out[0, 1] = from_left[1]
    out[3, 4] = from_right[...]
    for move in den_moves:
        move.wait_send()
    for pair in ten_moves + answers:
        for move in pair:
            move.wait_send()


def body(tensor, density, metric, offsets, counts):
    ring = lax.axis_size("row")
    hbm = pl.BlockSpec(memory_space=pltpu.HBM)
    return pl.pallas_call(
        functools.partial(kernel, ring),
        out_shape=jax.ShapeDtypeStruct(density.shape, F32),
        in_specs=[hbm] * 5,
        out_specs=pl.BlockSpec(memory_space=pltpu.VMEM),
        scratch_shapes=[
            pltpu.SMEM(metric.shape, F32),
            pltpu.SMEM(offsets.shape[::-1], jnp.int32),
            pltpu.SMEM(counts.shape, jnp.int32),
            pltpu.VMEM((BLOCKS, SLOTS, AUX, B, B), F32),
            pltpu.VMEM((BLOCKS, WIDTH, B, B), F32),
            pltpu.VMEM((3, B, B), F32),
            pltpu.VMEM((B, B), F32),
            pltpu.VMEM((3, B, B), F32),
            pltpu.VMEM((2, B, B), F32),
            pltpu.VMEM((SLOTS, AUX, B, B), F32),
            pltpu.VMEM((SLOTS, AUX, B, B), F32),
            pltpu.VMEM((ZERO + 1, B, B), BF16),
            pltpu.VMEM((ZERO + 1, B, B), BF16),
            pltpu.VMEM((BLOCKS, SLOTS + 1, 2, AUX * B, B), BF16),
            pltpu.VMEM((BLOCKS, SLOTS, B, AUX * B), BF16),
            pltpu.VMEM((BLOCKS, SLOTS, B, AUX * B), BF16),
            pltpu.VMEM((COLS, BLOCKS * B, AUX * B), BF16),
            pltpu.VMEM((COLS, BLOCKS * B, AUX * B), BF16),
            pltpu.VMEM((2, B, B), F32),
            pltpu.VMEM((B, B), F32),
            pltpu.VMEM((2, B, B), F32),
            pltpu.VMEM((B, B), F32),
            pltpu.SemaphoreType.DMA((5,)),
            pltpu.SemaphoreType.DMA((4 + 4 * CHUNKS,)),
            pltpu.SemaphoreType.DMA((4 + 4 * CHUNKS,)),
        ],
        compiler_params=pltpu.CompilerParams(
            collective_id=0, has_side_effects=True, vmem_limit_bytes=57 * 1024 * 1024
        ),
        cost_estimate=pl.CostEstimate(flops=6 * 10**9, bytes_accessed=6 * 10**6, transcendentals=0),
    )(tensor, density, metric, offsets.T, counts)


def solution(mesh):
    return jax.shard_map(
        body,
        mesh=mesh,
        in_specs=(
            P(("batch", "row"), None, None, None, None),
            P(("batch", "row"), None, None, None),
            P("batch", None),
            P("batch", None),
            P("batch"),
        ),
        out_specs=P(("batch", "row"), None, None, None),
        check_vma=False,
    )
```

```python
import functools

import jax
import jax.numpy as jnp
from jax import lax
from jax.experimental import pallas as pl
from jax.experimental.pallas import tpu as pltpu
from jax.sharding import PartitionSpec as P

MESH = pl.DeviceIdType.MESH
F32 = jnp.float32
BF16 = jnp.bfloat16
RADIUS = 2
WIDTH = 2 * RADIUS + 1
BLOCKS = 4
SLOTS = 3
AUX = 4
B = 128
ZERO = 8 * WIDTH
CHUNKS = 2
ROWS = B // CHUNKS
COLS = 13


def split(x):
    hi = x.astype(BF16)
    return hi, (x - hi.astype(F32)).astype(BF16)


def dot(a, b):
    return jnp.dot(a, b, preferred_element_type=F32)


def dot_t(a, b):
    return lax.dot_general(a, b, (((1,), (1,)), ((), ())), preferred_element_type=F32)


def kernel(
    ring,
    ten_hbm,
    den_hbm,
    metric_hbm,
    offsets_hbm,
    counts_hbm,
    out,
    metric,
    offsets,
    counts,
    ten,
    den,
    den_l3,
    den_l2,
    den_r0,
    den_r1,
    den_r2,
    pack_right,
    pack_left,
    ten_l,
    ten_r,
    d_hi,
    d_lo,
    v,
    u_hi,
    u_lo,
    e_hi,
    e_lo,
    to_right,
    to_left,
    from_left,
    from_right,
    local_sem,
    send_sem,
    recv_sem,
):
    me = lax.axis_index("row")
    right = lax.rem(me + 1, ring)
    left = lax.rem(me + ring - 1, ring)
    total = ring * BLOCKS
    first = me * BLOCKS

    own_ten = pltpu.make_async_copy(ten_hbm, ten, local_sem.at[0])
    own_den = pltpu.make_async_copy(den_hbm, den, local_sem.at[1])
    small = [
        pltpu.make_async_copy(src, dst, local_sem.at[2 + i])
        for i, (src, dst) in enumerate(
            ((metric_hbm, metric), (offsets_hbm, offsets), (counts_hbm, counts))
        )
    ]
    for move in small:
        move.start()
    own_den.start()
    own_ten.start()

    barrier = pltpu.get_barrier_semaphore()
    for side in (left, right):
        pl.semaphore_signal(barrier, inc=1, device_id={"row": side}, device_id_type=MESH)
    pl.semaphore_wait(barrier, 2)

    def remote(src, dst, number, side):
        return pltpu.make_async_remote_copy(
            src_ref=src,
            dst_ref=dst,
            send_sem=send_sem.at[number],
            recv_sem=recv_sem.at[number],
            device_id={"row": side},
            device_id_type=MESH,
        )

    den_moves = [
        remote(den_hbm.at[3, 0:2], den_l3, 0, right),
        remote(den_hbm.at[0, 3:5], den_r0, 1, left),
        remote(pack_right, den_l2, 2, right),
        remote(pack_left, den_r1, 3, left),
        remote(den_hbm.at[1, 3], den_r2, 4 + 4 * CHUNKS, left),
    ]
    rows_of = [pl.ds(c * ROWS, ROWS) for c in range(CHUNKS)]
    ten_moves = [
        [
            remote(ten_hbm.at[0, :, :, rows_of[c]], ten_r.at[:, :, rows_of[c]], 4 + 4 * c, left),
            remote(ten_hbm.at[3, :, :, rows_of[c]], ten_l.at[:, :, rows_of[c]], 5 + 4 * c, right),
        ]
        for c in range(CHUNKS)
    ]
    for number in (0, 1, 4):
        den_moves[number].start()

    row_of = lax.broadcasted_iota(jnp.int32, (B, B), 0)
    col_of = lax.broadcasted_iota(jnp.int32, (B, B), 1)

    def pack(buffer, one, two):
        buffer[0:B] = jnp.where(row_of >= col_of, one, two)
        diagonal = jnp.sum(jnp.where(row_of == col_of, two, 0.0), axis=0, keepdims=True)
        buffer[B : B + 8] = jnp.broadcast_to(diagonal, (8, B))

    def unpack(buffer):
        both = buffer[0:B]
        turned = both.T
        one = jnp.where(row_of >= col_of, both, turned)
        diagonal = jnp.broadcast_to(buffer[B : B + 1], (B, B))
        two = jnp.where(row_of < col_of, both, jnp.where(row_of > col_of, turned, diagonal))
        return one, two

    own_den.wait()
    pack(pack_right, den[3, 2], den[2, 2])
    pack(pack_left, den[0, 2], den[1, 2])
    den_moves[2].start()
    den_moves[3].start()
    for pair in ten_moves:
        for move in pair:
            move.start()
    answers = [
        [
            remote(to_right.at[:, rows_of[c]], from_left.at[:, rows_of[c]], 6 + 4 * c, right),
            remote(to_left.at[rows_of[c]], from_right.at[rows_of[c]], 7 + 4 * c, left),
        ]
        for c in range(CHUNKS)
    ]

    def block_offset(n, s):
        return offsets[s, lax.rem(first + n + total, total)]

    def block_live(n, s):
        return jnp.where(s < counts[lax.rem(first + n + total, total)], 1.0, 0.0).astype(F32)

    def put(i, k, block):
        hi, lo = split(block)
        d_hi[(i + RADIUS) * WIDTH + k] = hi
        d_lo[(i + RADIUS) * WIDTH + k] = lo

    for number in (0, 1, 2, 3, 5, 6, 7, 32, 33, 34, 36, 37, 38, 39, ZERO):
        d_hi[number] = jnp.zeros((B, B), BF16)
        d_lo[number] = jnp.zeros((B, B), BF16)

    def own_rows(step, carry):
        hi, lo = split(den[step])
        at = pl.ds((step + RADIUS) * WIDTH, WIDTH)
        d_hi[at] = hi
        d_lo[at] = lo
        return carry

    lax.fori_loop(0, BLOCKS, own_rows, 0)
    for i, j in ((-1, 0), (-1, 1), (-2, 0), (4, 2), (4, 3), (5, 3)):
        put(i, j - i + RADIUS, den[j, i - j + RADIUS].T)

    own_ten.wait()
    for move in small:
        move.wait()

    def prepare(m, carry):
        for s in range(SLOTS):
            live = block_live(m, s)
            parts = [ten[m, s, p] * live for p in range(AUX)]
            for q in range(AUX):
                hi, lo = split(parts[q])
                u_hi[m, s, :, q * B : (q + 1) * B] = hi
                u_lo[m, s, :, q * B : (q + 1) * B] = lo
                mixed = metric[q, 0] * parts[0]
                for p in range(1, AUX):
                    mixed = mixed + metric[q, p] * parts[p]
                hi, lo = split(mixed)
                v[m, s, 0, q * B : (q + 1) * B] = hi
                v[m, s, 1, q * B : (q + 1) * B] = lo
        v[m, SLOTS] = jnp.zeros((2, AUX * B, B), BF16)
        return carry

    lax.fori_loop(0, BLOCKS, prepare, 0)

    def half(m, o):
        rows_hi, rows_lo = [], []
        for s in range(SLOTS):
            shift = block_offset(m, s)
            pair_hi, pair_lo = [], []
            for step in (0, 1):
                k = o + step - shift + RADIUS
                at = jnp.where(
                    jnp.logical_and(k >= 0, k < WIDTH),
                    (m + shift + RADIUS) * WIDTH + k,
                    ZERO,
                )
                pair_hi.append(d_hi[at])
                pair_lo.append(d_lo[at])
            rows_hi.append(jnp.concatenate(pair_hi, axis=1))
            rows_lo.append(jnp.concatenate(pair_lo, axis=1))
        left_hi = [v[m, s, 0] for s in range(SLOTS)]
        left_lo = [v[m, s, 1] for s in range(SLOTS)]
        result = dot(
            jnp.concatenate(left_hi + left_hi + left_lo, axis=1),
            jnp.concatenate(rows_hi + rows_lo + rows_hi, axis=0),
        )
        rows = pl.ds(pl.multiple_of(m * B, B), B)
        for step in (0, 1):
            for q in range(AUX):
                hi, lo = split(result[q * B : (q + 1) * B, step * B : (step + 1) * B])
                e_hi[m + o + step + 4, rows, q * B : (q + 1) * B] = hi
                e_lo[m + o + step + 4, rows, q * B : (q + 1) * B] = lo

    def all_halves(number, carry):
        half(number // 4, (number % 4) * 2 - 2)
        return carry

    lax.fori_loop(0, 4 * BLOCKS, all_halves, 0)
    half(1, -4)

    def slot_at(m, shift):
        at = SLOTS
        for s in range(SLOTS):
            at = jnp.where(block_offset(m, s) == shift, s, at)
        return at

    def add_half(m, shifts, columns, blocks):
        ats = [slot_at(m, shift) for shift in shifts]
        left_hi = [v[m, at, 0] for at in ats]
        left_lo = [v[m, at, 1] for at in ats]
        rows_hi = [jnp.concatenate([b[0] for b in row], axis=1) for row in blocks]
        rows_lo = [jnp.concatenate([b[1] for b in row], axis=1) for row in blocks]
        result = dot(
            jnp.concatenate(left_hi + left_hi + left_lo, axis=1),
            jnp.concatenate(rows_hi + rows_lo + rows_hi, axis=0),
        )
        rows = slice(m * B, (m + 1) * B)
        for step, j in enumerate(columns):
            for q in range(AUX):
                lanes = slice(q * B, (q + 1) * B)
                old = e_hi[j + 4, rows, lanes].astype(F32) + e_lo[j + 4, rows, lanes].astype(F32)
                hi, lo = split(old + result[lanes, step * B : (step + 1) * B])
                e_hi[j + 4, rows, lanes] = hi
                e_lo[j + 4, rows, lanes] = lo

    for move in den_moves:
        move.wait_recv()
    near, far = unpack(den_l2)
    row_l1 = [split(den_l3[0]), split(den_l3[1]), split(near)]
    row_l2 = [split(far), split(den_l3[1].T)]
    add_half(0, (-1, -2), (-2, -1), [row_l1[1:], row_l2])
    add_half(1, (-2,), (-3, -2, -1), [row_l1])
    near, far = unpack(den_r1)
    row_r0 = [split(near), split(den_r0[0]), split(den_r0[1])]
    row_r1 = [split(den_r0[0].T), split(far), split(den_r2[...])]
    add_half(2, (2,), (4, 5, 6), [row_r0])
    add_half(3, (1, 2), (4, 5, 6), [row_r0, row_r1])

    def close(n, start, stop, part_hi, part_lo):
        result = jnp.zeros(((stop - start) * B, B), F32)
        for s in range(SLOTS):
            at = n + block_offset(n, s) + 4
            left_hi = e_hi[at, start * B : stop * B, :]
            left_lo = e_lo[at, start * B : stop * B, :]
            right_hi, right_lo = part_hi(s), part_lo(s)
            result = result + (
                dot_t(left_hi, right_hi) + (dot_t(left_hi, right_lo) + dot_t(left_lo, right_hi))
            )
        return [result[i * B : (i + 1) * B] for i in range(stop - start)]

    for n in range(BLOCKS):
        start = max(0, n - RADIUS)
        found = close(n, start, n + 1, lambda s: u_hi[n, s], lambda s: u_lo[n, s])
        for m in range(start, n + 1):
            block = found[m - start]
            out[m, n - m + RADIUS] = block
            if m < n:
                out[n, m - n + RADIUS] = block.T

    def close_arrived(buffer, n, start, stop, rows):
        result = jnp.zeros((ROWS, (stop - start) * B), F32)
        for s in range(SLOTS):
            live = block_live(n, s)
            pieces = [split(buffer[s, q, rows] * live) for q in range(AUX)]
            left_hi, left_lo = [
                jnp.concatenate([piece[i] for piece in pieces], axis=1) for i in (0, 1)
            ]
            at = n + block_offset(n, s) + 4
            right_hi = e_hi[at, start * B : stop * B, :]
            right_lo = e_lo[at, start * B : stop * B, :]
            result = result + (
                dot_t(left_hi, right_hi) + (dot_t(left_hi, right_lo) + dot_t(left_lo, right_hi))
            )
        return [result[:, i * B : (i + 1) * B] for i in range(stop - start)]

    for c in range(CHUNKS):
        rows = slice(c * ROWS, (c + 1) * ROWS)
        ten_moves[c][0].wait_recv()
        found = close_arrived(ten_r, 4, 2, 4, rows)
        for i in (0, 1):
            to_right[i, rows] = found[i]
        answers[c][0].start()
        ten_moves[c][1].wait_recv()
        (found,) = close_arrived(ten_l, -1, 1, 2, rows)
        to_left[rows] = found
        answers[c][1].start()

    for i in (0, 1):
        out[2 + i, 4 - i] = to_right[i].T
    out[1, 0] = to_left[...].T

    for pair in answers:
        for move in pair:
            move.wait_recv()
    out[0, 0] = from_left[0]
    out[0, 1] = from_left[1]
    out[3, 4] = from_right[...]
    for move in den_moves:
        move.wait_send()
    for pair in ten_moves + answers:
        for move in pair:
            move.wait_send()


def body(tensor, density, metric, offsets, counts):
    ring = lax.axis_size("row")
    hbm = pl.BlockSpec(memory_space=pltpu.HBM)
    return pl.pallas_call(
        functools.partial(kernel, ring),
        out_shape=jax.ShapeDtypeStruct(density.shape, F32),
        in_specs=[hbm] * 5,
        out_specs=pl.BlockSpec(memory_space=pltpu.VMEM),
        scratch_shapes=[
            pltpu.SMEM(metric.shape, F32),
            pltpu.SMEM(offsets.shape[::-1], jnp.int32),
            pltpu.SMEM(counts.shape, jnp.int32),
            pltpu.VMEM((BLOCKS, SLOTS, AUX, B, B), F32),
            pltpu.VMEM((BLOCKS, WIDTH, B, B), F32),
            pltpu.VMEM((2, B, B), F32),
            pltpu.VMEM((B + 8, B), F32),
            pltpu.VMEM((2, B, B), F32),
            pltpu.VMEM((B + 8, B), F32),
            pltpu.VMEM((B, B), F32),
            pltpu.VMEM((B + 8, B), F32),
            pltpu.VMEM((B + 8, B), F32),
            pltpu.VMEM((SLOTS, AUX, B, B), F32),
            pltpu.VMEM((SLOTS, AUX, B, B), F32),
            pltpu.VMEM((ZERO + 1, B, B), BF16),
            pltpu.VMEM((ZERO + 1, B, B), BF16),
            pltpu.VMEM((BLOCKS, SLOTS + 1, 2, AUX * B, B), BF16),
            pltpu.VMEM((BLOCKS, SLOTS, B, AUX * B), BF16),
            pltpu.VMEM((BLOCKS, SLOTS, B, AUX * B), BF16),
            pltpu.VMEM((COLS, BLOCKS * B, AUX * B), BF16),
            pltpu.VMEM((COLS, BLOCKS * B, AUX * B), BF16),
            pltpu.VMEM((2, B, B), F32),
            pltpu.VMEM((B, B), F32),
            pltpu.VMEM((2, B, B), F32),
            pltpu.VMEM((B, B), F32),
            pltpu.SemaphoreType.DMA((5,)),
            pltpu.SemaphoreType.DMA((5 + 4 * CHUNKS,)),
            pltpu.SemaphoreType.DMA((5 + 4 * CHUNKS,)),
        ],
        compiler_params=pltpu.CompilerParams(
            collective_id=0, has_side_effects=True, vmem_limit_bytes=57 * 1024 * 1024
        ),
        cost_estimate=pl.CostEstimate(flops=6 * 10**9, bytes_accessed=6 * 10**6, transcendentals=0),
    )(tensor, density, metric, offsets.T, counts)


def solution(mesh):
    return jax.shard_map(
        body,
        mesh=mesh,
        in_specs=(
            P(("batch", "row"), None, None, None, None),
            P(("batch", "row"), None, None, None),
            P("batch", None),
            P("batch", None),
            P("batch"),
        ),
        out_specs=P(("batch", "row"), None, None, None),
        check_vma=False,
    )
```

```python
import functools

import jax
import jax.numpy as jnp
from jax import lax
from jax.experimental import pallas as pl
from jax.experimental.pallas import tpu as pltpu
from jax.sharding import PartitionSpec as P

MESH = pl.DeviceIdType.MESH
F32 = jnp.float32
BF16 = jnp.bfloat16
RADIUS = 2
WIDTH = 2 * RADIUS + 1
BLOCKS = 4
SLOTS = 3
AUX = 4
B = 128
ZERO = 8 * WIDTH
CHUNKS = 2
ROWS = B // CHUNKS
COLS = 13


def split(x):
    hi = x.astype(BF16)
    return hi, (x - hi.astype(F32)).astype(BF16)


def dot(a, b):
    return jnp.dot(a, b, preferred_element_type=F32)


def dot_t(a, b):
    return lax.dot_general(a, b, (((1,), (1,)), ((), ())), preferred_element_type=F32)


def kernel(
    ring,
    ten_hbm,
    den_hbm,
    metric_hbm,
    offsets_hbm,
    counts_hbm,
    out_hbm,
    out,
    metric,
    offsets,
    counts,
    ten,
    den,
    den_l3,
    den_l2,
    den_r0,
    den_r1,
    den_r2,
    pack_right,
    pack_left,
    ten_l,
    ten_r,
    d_hi,
    d_lo,
    v,
    u_hi,
    u_lo,
    e_hi,
    e_lo,
    to_right,
    to_left,
    from_left,
    from_right,
    local_sem,
    send_sem,
    recv_sem,
    out_sem,
):
    me = lax.axis_index("row")
    right = lax.rem(me + 1, ring)
    left = lax.rem(me + ring - 1, ring)
    total = ring * BLOCKS
    first = me * BLOCKS

    own_ten = pltpu.make_async_copy(ten_hbm, ten, local_sem.at[0])
    own_den = pltpu.make_async_copy(den_hbm, den, local_sem.at[1])
    small = [
        pltpu.make_async_copy(src, dst, local_sem.at[2 + i])
        for i, (src, dst) in enumerate(
            ((metric_hbm, metric), (offsets_hbm, offsets), (counts_hbm, counts))
        )
    ]
    for move in small:
        move.start()
    own_den.start()
    own_ten.start()

    barrier = pltpu.get_barrier_semaphore()
    for side in (left, right):
        pl.semaphore_signal(barrier, inc=1, device_id={"row": side}, device_id_type=MESH)
    pl.semaphore_wait(barrier, 2)

    def remote(src, dst, number, side):
        return pltpu.make_async_remote_copy(
            src_ref=src,
            dst_ref=dst,
            send_sem=send_sem.at[number],
            recv_sem=recv_sem.at[number],
            device_id={"row": side},
            device_id_type=MESH,
        )

    den_moves = [
        remote(den_hbm.at[3, 0:2], den_l3, 0, right),
        remote(den_hbm.at[0, 3:5], den_r0, 1, left),
        remote(pack_right, den_l2, 2, right),
        remote(pack_left, den_r1, 3, left),
        remote(den_hbm.at[1, 3], den_r2, 4 + 4 * CHUNKS, left),
    ]
    rows_of = [pl.ds(c * ROWS, ROWS) for c in range(CHUNKS)]
    ten_moves = [
        [
            remote(ten_hbm.at[0, :, :, rows_of[c]], ten_r.at[:, :, rows_of[c]], 4 + 4 * c, left),
            remote(ten_hbm.at[3, :, :, rows_of[c]], ten_l.at[:, :, rows_of[c]], 5 + 4 * c, right),
        ]
        for c in range(CHUNKS)
    ]
    for number in (0, 1, 4):
        den_moves[number].start()

    row_of = lax.broadcasted_iota(jnp.int32, (B, B), 0)
    col_of = lax.broadcasted_iota(jnp.int32, (B, B), 1)

    def pack(buffer, one, two):
        buffer[0:B] = jnp.where(row_of >= col_of, one, two)
        diagonal = jnp.sum(jnp.where(row_of == col_of, two, 0.0), axis=0, keepdims=True)
        buffer[B : B + 8] = jnp.broadcast_to(diagonal, (8, B))

    def unpack(buffer):
        both = buffer[0:B]
        turned = both.T
        one = jnp.where(row_of >= col_of, both, turned)
        diagonal = jnp.broadcast_to(buffer[B : B + 1], (B, B))
        two = jnp.where(row_of < col_of, both, jnp.where(row_of > col_of, turned, diagonal))
        return one, two

    own_den.wait()
    pack(pack_right, den[3, 2], den[2, 2])
    pack(pack_left, den[0, 2], den[1, 2])
    den_moves[2].start()
    den_moves[3].start()
    for pair in ten_moves:
        for move in pair:
            move.start()
    answers = [
        [
            remote(to_right.at[:, rows_of[c]], from_left.at[:, rows_of[c]], 6 + 4 * c, right),
            remote(to_left.at[rows_of[c]], from_right.at[rows_of[c]], 7 + 4 * c, left),
        ]
        for c in range(CHUNKS)
    ]

    def block_offset(n, s):
        return offsets[s, lax.rem(first + n + total, total)]

    def block_live(n, s):
        return jnp.where(s < counts[lax.rem(first + n + total, total)], 1.0, 0.0).astype(F32)

    def put(i, k, block):
        hi, lo = split(block)
        d_hi[(i + RADIUS) * WIDTH + k] = hi
        d_lo[(i + RADIUS) * WIDTH + k] = lo

    for number in (0, 1, 2, 3, 5, 6, 7, 32, 33, 34, 36, 37, 38, 39, ZERO):
        d_hi[number] = jnp.zeros((B, B), BF16)
        d_lo[number] = jnp.zeros((B, B), BF16)

    def own_rows(step, carry):
        hi, lo = split(den[step])
        at = pl.ds((step + RADIUS) * WIDTH, WIDTH)
        d_hi[at] = hi
        d_lo[at] = lo
        return carry

    lax.fori_loop(0, BLOCKS, own_rows, 0)
    for i, j in ((-1, 0), (-1, 1), (-2, 0), (4, 2), (4, 3), (5, 3)):
        put(i, j - i + RADIUS, den[j, i - j + RADIUS].T)

    own_ten.wait()
    for move in small:
        move.wait()

    def prepare(m, carry):
        for s in range(SLOTS):
            live = block_live(m, s)
            parts = [ten[m, s, p] * live for p in range(AUX)]
            for q in range(AUX):
                hi, lo = split(parts[q])
                u_hi[m, s, :, q * B : (q + 1) * B] = hi
                u_lo[m, s, :, q * B : (q + 1) * B] = lo
                mixed = metric[q, 0] * parts[0]
                for p in range(1, AUX):
                    mixed = mixed + metric[q, p] * parts[p]
                hi, lo = split(mixed)
                v[m, s, 0, q * B : (q + 1) * B] = hi
                v[m, s, 1, q * B : (q + 1) * B] = lo
        v[m, SLOTS] = jnp.zeros((2, AUX * B, B), BF16)
        return carry

    lax.fori_loop(0, BLOCKS, prepare, 0)

    def half(m, o):
        rows_hi, rows_lo = [], []
        for s in range(SLOTS):
            shift = block_offset(m, s)
            pair_hi, pair_lo = [], []
            for step in (0, 1):
                k = o + step - shift + RADIUS
                at = jnp.where(
                    jnp.logical_and(k >= 0, k < WIDTH),
                    (m + shift + RADIUS) * WIDTH + k,
                    ZERO,
                )
                pair_hi.append(d_hi[at])
                pair_lo.append(d_lo[at])
            rows_hi.append(jnp.concatenate(pair_hi, axis=1))
            rows_lo.append(jnp.concatenate(pair_lo, axis=1))
        left_hi = [v[m, s, 0] for s in range(SLOTS)]
        left_lo = [v[m, s, 1] for s in range(SLOTS)]
        result = dot(
            jnp.concatenate(left_hi + left_hi + left_lo, axis=1),
            jnp.concatenate(rows_hi + rows_lo + rows_hi, axis=0),
        )
        rows = pl.ds(pl.multiple_of(m * B, B), B)
        for step in (0, 1):
            for q in range(AUX):
                hi, lo = split(result[q * B : (q + 1) * B, step * B : (step + 1) * B])
                e_hi[m + o + step + 4, rows, q * B : (q + 1) * B] = hi
                e_lo[m + o + step + 4, rows, q * B : (q + 1) * B] = lo

    def all_halves(number, carry):
        half(number // 4, (number % 4) * 2 - 2)
        return carry

    lax.fori_loop(0, 4 * BLOCKS, all_halves, 0)
    half(1, -4)

    def slot_at(m, shift):
        at = SLOTS
        for s in range(SLOTS):
            at = jnp.where(block_offset(m, s) == shift, s, at)
        return at

    def add_half(m, shifts, columns, blocks):
        ats = [slot_at(m, shift) for shift in shifts]
        left_hi = [v[m, at, 0] for at in ats]
        left_lo = [v[m, at, 1] for at in ats]
        rows_hi = [jnp.concatenate([b[0] for b in row], axis=1) for row in blocks]
        rows_lo = [jnp.concatenate([b[1] for b in row], axis=1) for row in blocks]
        result = dot(
            jnp.concatenate(left_hi + left_hi + left_lo, axis=1),
            jnp.concatenate(rows_hi + rows_lo + rows_hi, axis=0),
        )
        rows = slice(m * B, (m + 1) * B)
        for step, j in enumerate(columns):
            for q in range(AUX):
                lanes = slice(q * B, (q + 1) * B)
                old = e_hi[j + 4, rows, lanes].astype(F32) + e_lo[j + 4, rows, lanes].astype(F32)
                hi, lo = split(old + result[lanes, step * B : (step + 1) * B])
                e_hi[j + 4, rows, lanes] = hi
                e_lo[j + 4, rows, lanes] = lo

    for move in den_moves:
        move.wait_recv()
    near, far = unpack(den_l2)
    row_l1 = [split(den_l3[0]), split(den_l3[1]), split(near)]
    row_l2 = [split(far), split(den_l3[1].T)]
    add_half(0, (-1, -2), (-2, -1), [row_l1[1:], row_l2])
    add_half(1, (-2,), (-3, -2, -1), [row_l1])
    near, far = unpack(den_r1)
    row_r0 = [split(near), split(den_r0[0]), split(den_r0[1])]
    row_r1 = [split(den_r0[0].T), split(far), split(den_r2[...])]
    add_half(2, (2,), (4, 5, 6), [row_r0])
    add_half(3, (1, 2), (4, 5, 6), [row_r0, row_r1])

    def close(n, start, stop, part_hi, part_lo):
        result = jnp.zeros(((stop - start) * B, B), F32)
        for s in range(SLOTS):
            at = n + block_offset(n, s) + 4
            left_hi = e_hi[at, start * B : stop * B, :]
            left_lo = e_lo[at, start * B : stop * B, :]
            right_hi, right_lo = part_hi(s), part_lo(s)
            result = result + (
                dot_t(left_hi, right_hi) + (dot_t(left_hi, right_lo) + dot_t(left_lo, right_hi))
            )
        return [result[i * B : (i + 1) * B] for i in range(stop - start)]

    for n in range(BLOCKS):
        start = max(0, n - RADIUS)
        found = close(n, start, n + 1, lambda s: u_hi[n, s], lambda s: u_lo[n, s])
        for m in range(start, n + 1):
            block = found[m - start]
            out[m, n - m + RADIUS] = block
            if m < n:
                out[n, m - n + RADIUS] = block.T

    def close_arrived(buffer, n, start, stop, rows):
        result = jnp.zeros((ROWS, (stop - start) * B), F32)
        for s in range(SLOTS):
            live = block_live(n, s)
            pieces = [split(buffer[s, q, rows] * live) for q in range(AUX)]
            left_hi, left_lo = [
                jnp.concatenate([piece[i] for piece in pieces], axis=1) for i in (0, 1)
            ]
            at = n + block_offset(n, s) + 4
            right_hi = e_hi[at, start * B : stop * B, :]
            right_lo = e_lo[at, start * B : stop * B, :]
            result = result + (
                dot_t(left_hi, right_hi) + (dot_t(left_hi, right_lo) + dot_t(left_lo, right_hi))
            )
        return [result[:, i * B : (i + 1) * B] for i in range(stop - start)]

    def leave(number, m, start, stop):
        return pltpu.make_async_copy(
            out.at[m, start:stop], out_hbm.at[m, start:stop], out_sem.at[number]
        )

    early = [leave(0, 0, 2, 5), leave(1, 1, 1, 5), leave(2, 2, 0, 4), leave(3, 3, 0, 3)]
    late = [leave(4, 0, 0, 2), leave(5, 1, 0, 1), leave(6, 2, 4, 5), leave(7, 3, 3, 5)]
    for move in early:
        move.start()

    for c in range(CHUNKS):
        rows = slice(c * ROWS, (c + 1) * ROWS)
        ten_moves[c][0].wait_recv()
        found = close_arrived(ten_r, 4, 2, 4, rows)
        for i in (0, 1):
            to_right[i, rows] = found[i]
        answers[c][0].start()
        ten_moves[c][1].wait_recv()
        (found,) = close_arrived(ten_l, -1, 1, 2, rows)
        to_left[rows] = found
        answers[c][1].start()

    for i in (0, 1):
        out[2 + i, 4 - i] = to_right[i].T
    out[1, 0] = to_left[...].T
    late[1].start()
    late[2].start()

    for pair in answers:
        for move in pair:
            move.wait_recv()
    out[0, 0] = from_left[0]
    out[0, 1] = from_left[1]
    out[3, 4] = from_right[...]
    late[0].start()
    late[3].start()
    for move in early + late:
        move.wait()
    for move in den_moves:
        move.wait_send()
    for pair in ten_moves + answers:
        for move in pair:
            move.wait_send()


def body(tensor, density, metric, offsets, counts):
    ring = lax.axis_size("row")
    hbm = pl.BlockSpec(memory_space=pltpu.HBM)
    return pl.pallas_call(
        functools.partial(kernel, ring),
        out_shape=jax.ShapeDtypeStruct(density.shape, F32),
        in_specs=[hbm] * 5,
        out_specs=hbm,
        scratch_shapes=[
            pltpu.VMEM(density.shape, F32),
            pltpu.SMEM(metric.shape, F32),
            pltpu.SMEM(offsets.shape[::-1], jnp.int32),
            pltpu.SMEM(counts.shape, jnp.int32),
            pltpu.VMEM((BLOCKS, SLOTS, AUX, B, B), F32),
            pltpu.VMEM((BLOCKS, WIDTH, B, B), F32),
            pltpu.VMEM((2, B, B), F32),
            pltpu.VMEM((B + 8, B), F32),
            pltpu.VMEM((2, B, B), F32),
            pltpu.VMEM((B + 8, B), F32),
            pltpu.VMEM((B, B), F32),
            pltpu.VMEM((B + 8, B), F32),
            pltpu.VMEM((B + 8, B), F32),
            pltpu.VMEM((SLOTS, AUX, B, B), F32),
            pltpu.VMEM((SLOTS, AUX, B, B), F32),
            pltpu.VMEM((ZERO + 1, B, B), BF16),
            pltpu.VMEM((ZERO + 1, B, B), BF16),
            pltpu.VMEM((BLOCKS, SLOTS + 1, 2, AUX * B, B), BF16),
            pltpu.VMEM((BLOCKS, SLOTS, B, AUX * B), BF16),
            pltpu.VMEM((BLOCKS, SLOTS, B, AUX * B), BF16),
            pltpu.VMEM((COLS, BLOCKS * B, AUX * B), BF16),
            pltpu.VMEM((COLS, BLOCKS * B, AUX * B), BF16),
            pltpu.VMEM((2, B, B), F32),
            pltpu.VMEM((B, B), F32),
            pltpu.VMEM((2, B, B), F32),
            pltpu.VMEM((B, B), F32),
            pltpu.SemaphoreType.DMA((5,)),
            pltpu.SemaphoreType.DMA((5 + 4 * CHUNKS,)),
            pltpu.SemaphoreType.DMA((5 + 4 * CHUNKS,)),
            pltpu.SemaphoreType.DMA((8,)),
        ],
        compiler_params=pltpu.CompilerParams(
            collective_id=0, has_side_effects=True, vmem_limit_bytes=57 * 1024 * 1024
        ),
        cost_estimate=pl.CostEstimate(flops=6 * 10**9, bytes_accessed=6 * 10**6, transcendentals=0),
    )(tensor, density, metric, offsets.T, counts)


def solution(mesh):
    return jax.shard_map(
        body,
        mesh=mesh,
        in_specs=(
            P(("batch", "row"), None, None, None, None),
            P(("batch", "row"), None, None, None),
            P("batch", None),
            P("batch", None),
            P("batch"),
        ),
        out_specs=P(("batch", "row"), None, None, None),
        check_vma=False,
    )
```
